32 devices in a mesh: view: 4 (over y, x), block: 8 (over z, core).
Axes of the slice: x: 2, y: 2, z: 4, core: 2. Of those that a mesh axis runs over, the one named last changes fastest.
Arguments:
- estimate: float32 [128, 128, 256], P('block'), may hold values from 0.3 to 3
- observed: float32 [4, 128, 2, 128, 256], P('view', 'block'), may hold values from 0.2 to 5
- route_dest: int32 [4, 128], P('view', 'block'), may hold values from -1 to 7, as said below
- route_pos: int32 [4, 128], P('view', 'block'), may hold values from -1 to 15, as said below
- view_span: int32 [8, 2], P('view'), may hold values from 0 to 64, as said below
- view_count: int32 [64], P('block'), may hold values from 4 to 8, as said below
- psf_taps: float32 [8, 3, 31], P('view'), may hold values from 0 to 2, as said below
- view_weight: float32 [8], P('view'), may hold values from 1 to 4
Outputs:
- restored: float32 [128, 128, 256], P('block')
The draws below stay inside these ranges and needn't reach their ends.
Inputs may be any that keep to these rules, and one draw needn't show every extreme that they name: `route_dest`: in each view group, every brick of one of its views that lies inside that view's sub-volume stands in exactly one slot of the group's devices, with its owner block and position (view of the group times 8 plus brick of the block); other slots hold -1. One device's slots send at most 2 bricks to one block, and some device sends 2 to some block. `route_pos`: position of the slot's brick as described for route_dest, -1 together with it. `view_span`: each sub-volume lies within the 64 bricks and holds at least 32 of them; the first view of each view group spans all of them. `view_count`: equals the number of views whose span holds the brick. `psf_taps`: each kernel is positive.
All inputs are finite; a program needn't handle non-finite values.
Results may differ from the reference program's by a relative error of at most 0.0003.
Values sent between devices are 32-bit elements; how exact they have to be, the bound alone decides.
A program may use at most 128 MiB of HBM per device.

```python
import math
import jax
import jax.numpy as jnp
from jax import lax

VPG = 2
TAPS = 31
BX = 2
BPS = 8
ITERS = 2
NY = 128
NZ = 256
VIEWS = 8
BRICKS = 64
NX = 128
SLOTS = 16


def span_table(key):
    base = jax.random.fold_in(key, 7)
    groups = VIEWS // VPG
    lengths = jax.random.randint(jax.random.fold_in(base, 1), (groups, VPG - 1), BRICKS // 2, BRICKS + 1)
    starts = jax.random.randint(jax.random.fold_in(base, 2), (groups, VPG - 1), 0, BRICKS - lengths + 1)
    leading_full_block = jnp.zeros((groups, 1), jnp.int32)
    length_full = jnp.full((groups, 1), BRICKS, jnp.int32)
    firsts = jnp.concatenate([leading_full_block, starts.astype(jnp.int32)], axis=1)
    spans = jnp.concatenate([length_full, lengths.astype(jnp.int32)], axis=1)
    return jnp.stack([firsts, spans], axis=-1).reshape(VIEWS, 2).astype(jnp.int32)


def route_table(key):
    spans = span_table(key)
    groups = VIEWS // VPG
    blocks = BRICKS // BPS
    shifts = jax.random.randint(jax.random.fold_in(key, 21), (groups,), 0, blocks)
    perm_keys = jax.random.split(jax.random.fold_in(key, 22), groups * blocks)
    perms = jax.vmap(lambda single: jax.random.permutation(single, SLOTS))(perm_keys)
    perms = perms.reshape(groups, blocks, SLOTS).astype(jnp.int32)
    source = jnp.arange(blocks, dtype=jnp.int32)[None, :, None]
    dest = (source - perms - shifts.astype(jnp.int32)[:, None, None]) % blocks
    view = jnp.arange(groups, dtype=jnp.int32)[:, None, None] * VPG + perms // BPS
    brick = dest * BPS + perms % BPS
    span_first = spans[view, 0]
    span_length = spans[view, 1]
    inside = (brick >= span_first) & (brick < span_first + span_length)
    dest_out = jnp.where(inside, dest, -1).reshape(groups, blocks * SLOTS).astype(jnp.int32)
    pos_out = jnp.where(inside, perms, -1).reshape(groups, blocks * SLOTS).astype(jnp.int32)
    return (dest_out, pos_out)


def draw_route_dest(key, part):
    return route_table(key)[0]


def draw_route_pos(key, part):
    return route_table(key)[1]


def draw_view_span(key, part):
    return span_table(key)


def draw_view_count(key, part):
    spans = span_table(key)
    brick_index = jnp.arange(BRICKS, dtype=jnp.int32)
    inside = (brick_index[None, :] >= spans[:, 0:1]) & (brick_index[None, :] < spans[:, 0:1] + spans[:, 1:2])
    return jnp.sum(inside.astype(jnp.int32), axis=0).astype(jnp.int32)


def draw_psf_taps(key, part):
    base = jax.random.fold_in(key, 41)
    centred = jnp.arange(TAPS, dtype=jnp.float32) - float(TAPS // 2)
    across = jnp.exp(jax.random.uniform(jax.random.fold_in(base, 4), (VIEWS, 1), jnp.float32, jnp.log(3.0), jnp.log(6.0)))
    lateral = jnp.exp(jax.random.uniform(jax.random.fold_in(base, 1), (VIEWS, 1), jnp.float32, jnp.log(1.5), jnp.log(3.0)))
    axial = jnp.exp(jax.random.uniform(jax.random.fold_in(base, 2), (VIEWS, 1), jnp.float32, jnp.log(3.0), jnp.log(6.0)))
    jitter = jax.random.uniform(jax.random.fold_in(base, 3), (VIEWS, 3, TAPS), jnp.float32, -0.2, 0.2)
    sigma = jnp.concatenate([across, lateral, axial], axis=1)[:, :, None]
    peak = jnp.exp(-centred[None, None, :] ** 2 / (2.0 * sigma * sigma))
    pedestal = jnp.array([0.05, 0.0, 0.0], jnp.float32)[None, :, None]
    return (peak * jnp.exp(jitter) + pedestal).astype(jnp.float32)


def block_scale(stream_key, dims, cuts, smallest, top_value):
    loudness, own = 1.0, jax.random.fold_in(stream_key, 6)
    for position, blocks in cuts:
        heights = jnp.exp(jax.random.uniform(jax.random.fold_in(own, position), (blocks,), jnp.float32, smallest / len(cuts), top_value / len(cuts)))
        loudness = loudness * jnp.repeat(heights, dims[position] // blocks).reshape([-1 if axis == position else 1 for axis in range(len(dims))])
    return loudness


def setup_inputs(seed: int = 0) -> dict:
    splits = jax.random.split(jax.random.key(seed), 9)
    estimate = jnp.clip(jnp.exp(math.log(3.0) - 2.3025851 * jax.random.uniform(splits[0], (NX, NY, NZ), jnp.float32) ** block_scale(splits[0], (NX, NY, NZ), ((0, 8),), -0.2, 0.2)), 0.3, 3.0)
    observed = jnp.clip(jnp.exp(math.log(5.0) - 3.218876 * jax.random.uniform(splits[1], (VIEWS // VPG, BRICKS // BPS * SLOTS, BX, NY, NZ), jnp.float32) ** block_scale(splits[1], (VIEWS // VPG, BRICKS // BPS * SLOTS, BX, NY, NZ), ((0, 4), (1, 8)), -0.2, 0.2)), 0.2, 5.0)
    route_dest = draw_route_dest(jax.random.fold_in(splits[8], 71), 0)
    route_pos = draw_route_pos(jax.random.fold_in(splits[8], 71), 0)
    view_span = draw_view_span(jax.random.fold_in(splits[8], 71), 0)
    view_count = draw_view_count(jax.random.fold_in(splits[8], 71), 0)
    psf_taps = draw_psf_taps(jax.random.fold_in(splits[8], 71), 0)
    view_weight = jnp.clip(jnp.exp(math.log(4.0) - 1.3862944 * jax.random.uniform(splits[7], (VIEWS,), jnp.float32) ** block_scale(splits[7], (VIEWS,), ((0, 4),), -0.2, 0.2)), 1.0, 4.0)
    return dict(estimate=estimate, observed=observed, route_dest=route_dest, route_pos=route_pos, view_span=view_span, view_count=view_count, psf_taps=psf_taps, view_weight=view_weight)


def banded_blur_matrix(filter_tap_values, row_count, col_count, offset_base, orientation):
    tap_count = filter_tap_values.shape[-1]
    grid_shape = (row_count, col_count, tap_count)
    row_index = lax.broadcasted_iota(jnp.int32, grid_shape, 0)
    col_index = lax.broadcasted_iota(jnp.int32, grid_shape, 1)
    tap_index = lax.broadcasted_iota(jnp.int32, grid_shape, 2)
    selected_entries = (orientation * (row_index - col_index) + offset_base == tap_index).astype(jnp.float32)
    return jnp.einsum("ewq,gq->gew", selected_entries, filter_tap_values, precision=lax.Precision.HIGHEST)


def blur_x(current, filter_tap_values, reverse):
    reach = TAPS // 2
    padded = jnp.pad(current, ((reach, reach), (0, 0), (0, 0)))
    summed = jnp.zeros_like(current)
    for offset in range(TAPS):
        weight_index = TAPS - 1 - offset if reverse else offset
        summed = summed + filter_tap_values[weight_index] * padded[offset:offset + NX]
    return summed


def reference(estimate, observed, route_dest, route_pos, view_span, view_count, psf_taps, view_weight):
    highest = lax.Precision.HIGHEST
    reach = TAPS // 2
    point_spread_kernels = psf_taps / jnp.sum(psf_taps, axis=-1, keepdims=True)
    mat_y = banded_blur_matrix(point_spread_kernels[:, 1], NY, NY, reach, 1)
    mat_z = banded_blur_matrix(point_spread_kernels[:, 2], NZ, NZ, reach, 1)
    brick_index = jnp.arange(BRICKS, dtype=jnp.int32)
    span_first = view_span[:, 0:1]
    span_length = view_span[:, 1:2]
    inside = ((brick_index[None, :] >= span_first) & (brick_index[None, :] < span_first + span_length)).astype(jnp.float32)
    live_cells = jnp.repeat(inside, BX, axis=1)
    counts = jnp.repeat(view_count.astype(jnp.float32), BX)[:, None, None]
    groups = VIEWS // VPG

    def group_obs(group):
        dest_list = route_dest[group]
        pos_list = route_pos[group]
        target = jnp.where(dest_list >= 0, (pos_list // BPS) * BRICKS + dest_list * BPS + pos_list % BPS, VPG * BRICKS)
        placed = jnp.zeros((VPG * BRICKS, BX, NY, NZ), jnp.float32).at[target].set(observed[group], mode="drop")
        return placed.reshape(VPG, NX, NY, NZ)

    current = estimate
    for iteration in range(ITERS):
        def add_group(summed, group):
            obs_views = group_obs(group)
            for local in range(VPG):
                view = group * VPG + local
                tap_x = point_spread_kernels[view, 0]
                blurred = blur_x(current, tap_x, False)
                blurred = jnp.einsum("xyz,yq->xqz", blurred, mat_y[view], precision=highest)
                blurred = jnp.einsum("xyz,zq->xyq", blurred, mat_z[view], precision=highest)
                cell_mask = live_cells[view][:, None, None]
                ratios = cell_mask * (obs_views[local] / blurred) + (1.0 - cell_mask)
                back = jnp.einsum("xyz,qz->xyq", ratios, mat_z[view], precision=highest)
                back = jnp.einsum("xyz,qy->xqz", back, mat_y[view], precision=highest)
                corrected = blur_x(back, tap_x, True)
                summed = summed + cell_mask * view_weight[view] * jnp.log(corrected)
            return summed, None

        summed, unused = lax.scan(add_group, jnp.zeros_like(current), jnp.arange(groups, dtype=jnp.int32))
        current = current * jnp.exp(summed / counts)
    return current
```

```python
import functools

import jax
import jax.numpy as jnp
from jax import lax
from jax.experimental import pallas as pl
from jax.experimental.pallas import tpu as pltpu
from jax.sharding import PartitionSpec as P

ITERS = 2
PREC = lax.Precision.HIGH


def with_halo(cells, sides, width):
    for axis, dim in sides:
        count = lax.axis_size(axis)
        ends = count - 1
        head = lax.slice_in_dim(cells, 0, width, axis=dim)
        tail = lax.slice_in_dim(cells, cells.shape[dim] - width, cells.shape[dim], axis=dim)
        cells = jnp.concatenate(
            [
                lax.ppermute(tail, axis, [(i, (i + 1) % count) for i in range(ends)]),
                cells,
                lax.ppermute(head, axis, [((i + 1) % count, i) for i in range(ends)]),
            ],
            axis=dim,
        )
    return cells


MESH = pl.DeviceIdType.MESH


def blur_tile(src, lead, taps_ref, view, rows, lanes, depth, first, step):
    total = None
    for t in range(taps_ref.shape[1]):
        start = first + step * t
        term = taps_ref[view, t] * src[(*lead, pl.ds(start, depth), rows, lanes)]
        total = term if total is None else total + term
    return total


def correct_kernel(last, reach, base, *refs):
    if last:
        (back_ref, f_ref, taps_ref, wm_ref, inv_ref, fout_ref,
         ext, own, part, rs, in_sem, rh_send, rh_recv, rs_send, rs_recv, ag_send, ag_recv) = refs
        fb, fbase = fout_ref, 0
    else:
        (back_ref, f_ref, taps_ref, wm_ref, inv_ref, fout_ref, along_ref,
         ext, own, part, rs, in_sem, rh_send, rh_recv, rs_send, rs_recv, ag_send, ag_recv,
         fext, fh_send, fh_recv) = refs
        fb, fbase = fext, reach + 1
    views, depth = back_ref.shape[0], back_ref.shape[1]
    ny, nz = back_ref.shape[2], back_ref.shape[3]
    pad = reach + 1
    group = lax.axis_size("view")
    blocks = lax.axis_size("block")
    me = lax.axis_index("view")
    blk = lax.axis_index("block")
    piece = ny // group
    has_left = blk > 0
    has_right = blk < blocks - 1

    def rows_of(p):
        return pl.ds(pl.multiple_of(p * piece, piece), piece)

    centre = pltpu.make_async_copy(back_ref, ext.at[:, pl.ds(pad, depth)], in_sem.at[0])
    centre.start()
    mine = pltpu.make_async_copy(
        f_ref.at[:, rows_of(me)], own, in_sem.at[1]
    )
    mine.start()

    barrier = pltpu.get_barrier_semaphore()
    for s in range(group - 1):
        pl.semaphore_signal(
            barrier, inc=1, device_id=(lax.rem(me + 1 + s, group), blk), device_id_type=MESH
        )

    @pl.when(has_left)
    def _():
        pl.semaphore_signal(barrier, inc=1, device_id=(me, blk - 1), device_id_type=MESH)

    @pl.when(has_right)
    def _():
        pl.semaphore_signal(barrier, inc=1, device_id=(me, blk + 1), device_id_type=MESH)

    @pl.when(blk == 0)
    def _():
        ext[:, 0:pad] = jnp.zeros((views, pad, ny, nz), jnp.float32)
        if not last:
            fext[0:pad] = jnp.zeros((pad, ny, nz), jnp.float32)

    @pl.when(blk == blocks - 1)
    def _():
        ext[:, pad + depth:] = jnp.zeros((views, pad, ny, nz), jnp.float32)
        if not last:
            fext[pad + depth:] = jnp.zeros((pad, ny, nz), jnp.float32)

    pl.semaphore_wait(
        barrier, group - 1 + has_left.astype(jnp.int32) + has_right.astype(jnp.int32)
    )
    centre.wait()

    def ratio_copy(side, s):
        rows = rows_of(lax.rem(me + 1 + s, group))
        src0, dst0 = (pad + depth - reach, pad - reach) if side == 0 else (pad, pad + depth)
        return pltpu.make_async_remote_copy(
            src_ref=ext.at[:, pl.ds(src0, reach), rows],
            dst_ref=ext.at[:, pl.ds(dst0, reach), rows],
            send_sem=rh_send.at[side, s],
            recv_sem=rh_recv.at[side, s],
            device_id=(me, blk + 1 if side == 0 else blk - 1),
            device_id_type=MESH,
        )

    def field_copy(side, k):
        p = me if k == 0 else lax.rem(me - k + group, group)
        rows = rows_of(p)
        src0, dst0 = (pad + depth - reach, pad - reach) if side == 0 else (pad, pad + depth)
        return pltpu.make_async_remote_copy(
            src_ref=fext.at[pl.ds(src0, reach), rows],
            dst_ref=fext.at[pl.ds(dst0, reach), rows],
            send_sem=fh_send.at[side, k],
            recv_sem=fh_recv.at[side, k],
            device_id=(me, blk + 1 if side == 0 else blk - 1),
            device_id_type=MESH,
        )

    def to_sides(make, k, act):
        @pl.when(has_right)
        def _():
            act(make(0, k))

        @pl.when(has_left)
        def _():
            act(make(1, k))

    def from_sides(make, k):
        @pl.when(has_left)
        def _():
            make(0, k).wait_recv()

        @pl.when(has_right)
        def _():
            make(1, k).wait_recv()

    for s in range(group):
        to_sides(ratio_copy, s, lambda c: c.start())

    tiles = (piece // 8) * (nz // 128)

    def tile_at(p, i):
        rows = pl.ds(pl.multiple_of(p * piece + (i // (nz // 128)) * 8, 8), 8)
        inner = pl.ds(pl.multiple_of((i // (nz // 128)) * 8, 8), 8)
        lanes = pl.ds(pl.multiple_of((i % (nz // 128)) * 128, 128), 128)
        return rows, inner, lanes

    def sum_copy(s):
        return pltpu.make_async_remote_copy(
            src_ref=part.at[s],
            dst_ref=rs.at[s],
            send_sem=rs_send.at[s],
            recv_sem=rs_recv.at[s],
            device_id=(lax.rem(me + 1 + s, group), blk),
            device_id_type=MESH,
        )

    for s in range(group):
        p = lax.rem(me + 1 + s, group)
        from_sides(ratio_copy, s)

        def body(i, carry, p=p, s=s):
            rows, inner, lanes = tile_at(p, i)
            logs = [
                jnp.log(
                    blur_tile(ext, (v,), taps_ref, v, rows, lanes, depth, pad + reach, -1)
                )
                for v in range(views)
            ]
            for x in range(depth):
                total = wm_ref[0, x] * logs[0][x]
                for v in range(1, views):
                    total = total + wm_ref[v, x] * logs[v][x]
                part[s, x, inner, lanes] = total
            return carry

        lax.fori_loop(0, tiles, body, 0)
        if s < group - 1:
            sum_copy(s).start()

    mine.wait()
    for s in range(group - 1):
        sum_copy(s).wait_recv()

    def update(i, carry):
        rows, inner, lanes = tile_at(me, i)
        for x in range(depth):
            total = part[group - 1, x, inner, lanes]
            for s in range(group - 1):
                total = total + rs[s, x, inner, lanes]
            fb[fbase + x, rows, lanes] = own[x, inner, lanes] * jnp.exp(total * inv_ref[0, x])
        return carry

    lax.fori_loop(0, tiles, update, 0)

    def field_out(s):
        where = fb.at[pl.ds(fbase, depth), rows_of(me)]
        return pltpu.make_async_remote_copy(
            src_ref=where,
            dst_ref=where,
            send_sem=ag_send.at[s],
            recv_sem=ag_recv.at[s],
            device_id=(lax.rem(me + 1 + s, group), blk),
            device_id_type=MESH,
        )

    def field_in(s):
        where = fb.at[pl.ds(fbase, depth), rows_of(lax.rem(me - 1 - s + group, group))]
        return pltpu.make_async_remote_copy(
            src_ref=where,
            dst_ref=where,
            send_sem=ag_send.at[s],
            recv_sem=ag_recv.at[s],
            device_id=(lax.rem(me + 1 + s, group), blk),
            device_id_type=MESH,
        )

    for s in range(group - 1):
        field_out(s).start()
    if not last:
        to_sides(field_copy, 0, lambda c: c.start())
    for s in range(group - 1):
        field_in(s).wait_recv()
        if not last:
            to_sides(field_copy, s + 1, lambda c: c.start())
    if not last:
        done = pltpu.make_async_copy(fext.at[pl.ds(pad, depth)], fout_ref, in_sem.at[2])
        done.start()
        for k in range(group):
            p = me if k == 0 else lax.rem(me - k + group, group)
            from_sides(field_copy, k)

            def forward(i, carry, p=p):
                rows, _, lanes = tile_at(p, i)
                for v in range(views):
                    along_ref[v, :, rows, lanes] = blur_tile(
                        fext, (), taps_ref, v, rows, lanes, depth, pad - reach, 1
                    )
                return carry

            lax.fori_loop(0, tiles, forward, 0)
        done.wait()
        for k in range(group):
            to_sides(field_copy, k, lambda c: c.wait_send())
    for s in range(group):
        to_sides(ratio_copy, s, lambda c: c.wait_send())
    for s in range(group - 1):
        sum_copy(s).wait_send()
        field_out(s).wait_send()


def correct(back, field, taps, wm, inv, last):
    views, depth, ny, nz = back.shape
    group = lax.axis_size("view")
    reach = taps.shape[-1] // 2
    pad = reach + 1
    piece = ny // group
    dma = pltpu.SemaphoreType.DMA
    smem = pl.BlockSpec(memory_space=pltpu.SMEM)
    anywhere = pl.BlockSpec(memory_space=pl.ANY)
    vmem = pl.BlockSpec(memory_space=pltpu.VMEM)
    scratch = [
        pltpu.VMEM((views, depth + 2 * pad, ny, nz), jnp.float32),
        pltpu.VMEM((depth, piece, nz), jnp.float32),
        pltpu.VMEM((group, depth, piece, nz), jnp.float32),
        pltpu.VMEM((max(1, group - 1), depth, piece, nz), jnp.float32),
        dma((3,)),
        dma((2, group)),
        dma((2, group)),
        dma((group,)),
        dma((group,)),
        dma((group,)),
        dma((group,)),
    ]
    field_shape = jax.ShapeDtypeStruct((depth, ny, nz), jnp.float32)
    along_shape = jax.ShapeDtypeStruct((views, depth, ny, nz), jnp.float32)
    if not last:
        scratch += [
            pltpu.VMEM((depth + 2 * pad, ny, nz), jnp.float32), dma((2, group)), dma((2, group))
        ]
    return pl.pallas_call(
        functools.partial(correct_kernel, last, reach, 0),
        out_shape=field_shape if last else (field_shape, along_shape),
        in_specs=[anywhere, anywhere, smem, smem, smem],
        out_specs=vmem if last else (anywhere, vmem),
        scratch_shapes=scratch,
        compiler_params=pltpu.CompilerParams(
            collective_id=1 if last else 0,
            has_side_effects=True,
            vmem_limit_bytes=48 * 1024 * 1024,
        ),
        name="correct_last" if last else "correct_mid",
    )(back, field, taps, wm, inv)


def banded_blur_matrix(filter_tap_values, row_count, col_count, offset_base, orientation):
    tap_count = filter_tap_values.shape[-1]
    grid_shape = (row_count, col_count, tap_count)
    row_index = lax.broadcasted_iota(jnp.int32, grid_shape, 0)
    col_index = lax.broadcasted_iota(jnp.int32, grid_shape, 1)
    tap_index = lax.broadcasted_iota(jnp.int32, grid_shape, 2)
    selected_entries = (orientation * (row_index - col_index) + offset_base == tap_index).astype(
        jnp.float32
    )
    return jnp.einsum(
        "ewq,gq->gew", selected_entries, filter_tap_values, precision=lax.Precision.HIGHEST
    )


def on_device(
    estimate, observed, route_dest, route_pos, view_span, view_count, psf_taps, view_weight
):
    highest = lax.Precision.HIGHEST
    blocks = lax.axis_size("block")
    slot_count = observed.shape[1]
    planes = observed.shape[2]
    ny_cells = observed.shape[3]
    nz_cells = observed.shape[4]
    per_group = view_span.shape[0]
    per_block = view_count.shape[0]
    capacity = max(1, slot_count // blocks)
    block_x = per_block * planes
    reach = psf_taps.shape[-1] // 2
    sources = observed[0]
    dest_list = route_dest[0]
    pos_list = route_pos[0]
    slot_index = jnp.arange(slot_count, dtype=jnp.int32)
    earlier = (dest_list[:, None] == dest_list[None, :]) & (
        slot_index[None, :] < slot_index[:, None]
    )
    rank_in_dest = jnp.sum(earlier.astype(jnp.int32), axis=1)
    target = jnp.where(dest_list >= 0, dest_list * capacity + rank_in_dest, blocks * capacity)
    outgoing = (
        jnp.zeros((blocks * capacity, planes, ny_cells, nz_cells), jnp.float32)
        .at[target]
        .set(sources, mode="drop")
    )
    out_pos = (
        jnp.full((blocks * capacity,), -1.0, jnp.float32)
        .at[target]
        .set(pos_list.astype(jnp.float32), mode="drop")
    )
    arrived, arrived_pos = (
        lax.all_to_all(
            outgoing.reshape(blocks, capacity, planes, ny_cells, nz_cells),
            "block",
            split_axis=0,
            concat_axis=0,
            tiled=True,
        ),
        lax.all_to_all(
            out_pos.reshape(blocks, capacity), "block", split_axis=0, concat_axis=0, tiled=True
        ),
    )
    places = arrived_pos.reshape(-1).astype(jnp.int32)
    places = jnp.where(places >= 0, places, per_group * per_block)
    placed = (
        jnp.zeros((per_group * per_block, planes, ny_cells, nz_cells), jnp.float32)
        .at[places]
        .set(arrived.reshape(-1, planes, ny_cells, nz_cells), mode="drop")
    )
    obs_views = placed.reshape(per_group, block_x, ny_cells, nz_cells)
    brick_index = lax.axis_index("block") * per_block + jnp.arange(per_block, dtype=jnp.int32)
    span_first = view_span[:, 0:1]
    span_length = view_span[:, 1:2]
    inside = (
        (brick_index[None, :] >= span_first) & (brick_index[None, :] < span_first + span_length)
    ).astype(jnp.float32)
    live_cells = jnp.repeat(inside, planes, axis=1)[:, :, None, None]
    point_spread_kernels = psf_taps / jnp.sum(psf_taps, axis=-1, keepdims=True)
    fwd_x = banded_blur_matrix(point_spread_kernels[:, 0], block_x + 2 * reach, block_x, 0, 1)
    mat_y = banded_blur_matrix(point_spread_kernels[:, 1], ny_cells, ny_cells, reach, 1)
    mat_z = banded_blur_matrix(point_spread_kernels[:, 2], nz_cells, nz_cells, reach, 1)
    wm = jnp.repeat(inside, planes, axis=1) * view_weight[:, None]
    inv = (1.0 / jnp.repeat(view_count.astype(jnp.float32), planes))[None, :]
    taps_x = point_spread_kernels[:, 0]
    current = estimate
    padded = with_halo(current, (("block", 0),), reach)
    along_x = jnp.einsum("wyz,vwx->vxyz", padded, fwd_x, precision=highest)
    for iteration in range(ITERS):
        lateral_y_pass = jnp.einsum("vxyz,vyq->vxqz", along_x, mat_y, precision=PREC)
        blurred = jnp.einsum("vxyz,vzq->vxyq", lateral_y_pass, mat_z, precision=PREC)
        ratios = live_cells * (obs_views / blurred) + (1.0 - live_cells)
        back_z = jnp.einsum("vxyz,vqz->vxyq", ratios, mat_z, precision=PREC)
        back_y = jnp.einsum("vxyz,vqy->vxqz", back_z, mat_y, precision=PREC)
        if iteration < ITERS - 1:
            current, along_x = correct(back_y, current, taps_x, wm, inv, False)
        else:
            current = correct(back_y, current, taps_x, wm, inv, True)
    return current


def solution(mesh):
    placed = (
        P("block", None, None),
        P("view", "block", None, None, None),
        P("view", "block"),
        P("view", "block"),
        P("view", None),
        P("block"),
        P("view", None, None),
        P("view"),
    )
    return jax.shard_map(
        on_device, mesh=mesh, in_specs=placed, out_specs=P("block", None, None), check_vma=False
    )
```

```python
import functools

import jax
import jax.numpy as jnp
from jax import lax
from jax.experimental import pallas as pl
from jax.experimental.pallas import tpu as pltpu
from jax.sharding import PartitionSpec as P

ITERS = 2
PREC = lax.Precision.HIGH


def with_halo(cells, sides, width):
    for axis, dim in sides:
        count = lax.axis_size(axis)
        ends = count - 1
        head = lax.slice_in_dim(cells, 0, width, axis=dim)
        tail = lax.slice_in_dim(cells, cells.shape[dim] - width, cells.shape[dim], axis=dim)
        cells = jnp.concatenate(
            [
                lax.ppermute(tail, axis, [(i, (i + 1) % count) for i in range(ends)]),
                cells,
                lax.ppermute(head, axis, [((i + 1) % count, i) for i in range(ends)]),
            ],
            axis=dim,
        )
    return cells


MESH = pl.DeviceIdType.MESH


def blur_tile(src, lead, taps_ref, view, rows, lanes, depth, first, step):
    total = None
    for t in range(taps_ref.shape[1]):
        start = first + step * t
        term = taps_ref[view, t] * src[(*lead, pl.ds(start, depth), rows, lanes)]
        total = term if total is None else total + term
    return total


def correct_kernel(last, reach, *refs):
    if last:
        (back_ref, f_ref, taps_ref, wm_ref, inv_ref, fout_ref,
         ext, own, part, rs, in_sem, rh_send, rh_recv, rs_send, rs_recv, ag_send, ag_recv) = refs
        fb, fbase = fout_ref, 0
    else:
        (back_ref, f_ref, taps_ref, wm_ref, inv_ref, fout_ref, along_ref,
         ext, own, part, rs, in_sem, rh_send, rh_recv, rs_send, rs_recv, ag_send, ag_recv,
         fext, fh_send, fh_recv) = refs
        fb, fbase = fext, reach + 1
    views, depth = back_ref.shape[0], back_ref.shape[1]
    ny, nz = back_ref.shape[2], back_ref.shape[3]
    pad = reach + 1
    group = lax.axis_size("view")
    blocks = lax.axis_size("block")
    me = lax.axis_index("view")
    blk = lax.axis_index("block")
    piece = ny // group
    has_left = blk > 0
    has_right = blk < blocks - 1

    part_rows = 8
    rounds = piece // part_rows

    def rows_of(p):
        return pl.ds(pl.multiple_of(p * piece, piece), piece)

    def rows_at(p, r):
        return pl.ds(pl.multiple_of(p * piece + r * part_rows, part_rows), part_rows)

    def inner_at(r):
        return pl.ds(pl.multiple_of(r * part_rows, part_rows), part_rows)

    centre = pltpu.make_async_copy(back_ref, ext.at[:, pl.ds(pad, depth)], in_sem.at[0])
    centre.start()
    mine = pltpu.make_async_copy(
        f_ref.at[:, rows_of(me)], own, in_sem.at[1]
    )
    mine.start()

    barrier = pltpu.get_barrier_semaphore()
    for s in range(group - 1):
        pl.semaphore_signal(
            barrier, inc=1, device_id=(lax.rem(me + 1 + s, group), blk), device_id_type=MESH
        )

    @pl.when(has_left)
    def _():
        pl.semaphore_signal(barrier, inc=1, device_id=(me, blk - 1), device_id_type=MESH)

    @pl.when(has_right)
    def _():
        pl.semaphore_signal(barrier, inc=1, device_id=(me, blk + 1), device_id_type=MESH)

    @pl.when(blk == 0)
    def _():
        ext[:, 0:pad] = jnp.zeros((views, pad, ny, nz), jnp.float32)
        if not last:
            fext[0:pad] = jnp.zeros((pad, ny, nz), jnp.float32)

    @pl.when(blk == blocks - 1)
    def _():
        ext[:, pad + depth:] = jnp.zeros((views, pad, ny, nz), jnp.float32)
        if not last:
            fext[pad + depth:] = jnp.zeros((pad, ny, nz), jnp.float32)

    pl.semaphore_wait(
        barrier, group - 1 + has_left.astype(jnp.int32) + has_right.astype(jnp.int32)
    )
    centre.wait()

    def ratio_copy(side, s, r):
        rows = rows_at(lax.rem(me + 1 + s, group), r)
        src0, dst0 = (pad + depth - reach, pad - reach) if side == 0 else (pad, pad + depth)
        return pltpu.make_async_remote_copy(
            src_ref=ext.at[:, pl.ds(src0, reach), rows],
            dst_ref=ext.at[:, pl.ds(dst0, reach), rows],
            send_sem=rh_send.at[side, s, r],
            recv_sem=rh_recv.at[side, s, r],
            device_id=(me, blk + 1 if side == 0 else blk - 1),
            device_id_type=MESH,
        )

    def field_copy(side, k, r):
        p = me if k == 0 else lax.rem(me - k + group, group)
        rows = rows_at(p, r)
        src0, dst0 = (pad + depth - reach, pad - reach) if side == 0 else (pad, pad + depth)
        return pltpu.make_async_remote_copy(
            src_ref=fext.at[pl.ds(src0, reach), rows],
            dst_ref=fext.at[pl.ds(dst0, reach), rows],
            send_sem=fh_send.at[side, k, r],
            recv_sem=fh_recv.at[side, k, r],
            device_id=(me, blk + 1 if side == 0 else blk - 1),
            device_id_type=MESH,
        )

    def to_sides(make, k, r, act):
        @pl.when(has_right)
        def _():
            act(make(0, k, r))

        @pl.when(has_left)
        def _():
            act(make(1, k, r))

    def from_sides(make, k, r):
        @pl.when(has_left)
        def _():
            make(0, k, r).wait_recv()

        @pl.when(has_right)
        def _():
            make(1, k, r).wait_recv()

    def each_round(act):
        def step(r, carry):
            act(r)
            return carry

        lax.fori_loop(0, rounds, step, 0)

    @each_round
    def _(r):
        for s in range(group):
            to_sides(ratio_copy, s, r, lambda c: c.start())

    tiles = nz // 128

    def lanes_at(i):
        return pl.ds(pl.multiple_of(i * 128, 128), 128)

    def sum_copy(s, r):
        return pltpu.make_async_remote_copy(
            src_ref=part.at[s, :, inner_at(r)],
            dst_ref=rs.at[s, :, inner_at(r)],
            send_sem=rs_send.at[s, r],
            recv_sem=rs_recv.at[s, r],
            device_id=(lax.rem(me + 1 + s, group), blk),
            device_id_type=MESH,
        )

    def field_copy_to(s, r, p):
        where = fb.at[pl.ds(fbase, depth), rows_at(p, r)]
        return pltpu.make_async_remote_copy(
            src_ref=where,
            dst_ref=where,
            send_sem=ag_send.at[s, r],
            recv_sem=ag_recv.at[s, r],
            device_id=(lax.rem(me + 1 + s, group), blk),
            device_id_type=MESH,
        )

    def take_gathered(r):
        for s in range(group - 1):
            field_copy_to(s, r, lax.rem(me - 1 - s + group, group)).wait_recv()
            if not last:
                to_sides(field_copy, s + 1, r, lambda c: c.start())

    mine.wait()

    @each_round
    def _(r):
        inner = inner_at(r)
        for s in range(group):
            rows = rows_at(lax.rem(me + 1 + s, group), r)
            from_sides(ratio_copy, s, r)

            def body(i, carry, rows=rows, s=s):
                lanes = lanes_at(i)
                logs = [
                    jnp.log(
                        blur_tile(ext, (v,), taps_ref, v, rows, lanes, depth, pad + reach, -1)
                    )
                    for v in range(views)
                ]
                for x in range(depth):
                    total = wm_ref[0, x] * logs[0][x]
                    for v in range(1, views):
                        total = total + wm_ref[v, x] * logs[v][x]
                    part[s, x, inner, lanes] = total
                return carry

            lax.fori_loop(0, tiles, body, 0)
            if s < group - 1:
                sum_copy(s, r).start()

        for s in range(group - 1):
            sum_copy(s, r).wait_recv()
        rows = rows_at(me, r)

        def update(i, carry):
            lanes = lanes_at(i)
            for x in range(depth):
                total = part[group - 1, x, inner, lanes]
                for s in range(group - 1):
                    total = total + rs[s, x, inner, lanes]
                fb[fbase + x, rows, lanes] = own[x, inner, lanes] * jnp.exp(
                    total * inv_ref[0, x]
                )
            return carry

        lax.fori_loop(0, tiles, update, 0)
        for s in range(group - 1):
            field_copy_to(s, r, me).start()
        if not last:
            to_sides(field_copy, 0, r, lambda c: c.start())

        @pl.when(r > 0)
        def _():
            take_gathered(r - 1)

    take_gathered(rounds - 1)
    if not last:
        done = pltpu.make_async_copy(fext.at[pl.ds(pad, depth)], fout_ref, in_sem.at[2])
        done.start()

        @each_round
        def _(r):
            for k in range(group):
                rows = rows_at(me if k == 0 else lax.rem(me - k + group, group), r)
                from_sides(field_copy, k, r)

                def forward(i, carry, rows=rows):
                    lanes = lanes_at(i)
                    for v in range(views):
                        along_ref[v, :, rows, lanes] = blur_tile(
                            fext, (), taps_ref, v, rows, lanes, depth, pad - reach, 1
                        )
                    return carry

                lax.fori_loop(0, tiles, forward, 0)

        done.wait()

    @each_round
    def _(r):
        for s in range(group):
            to_sides(ratio_copy, s, r, lambda c: c.wait_send())
            if not last:
                to_sides(field_copy, s, r, lambda c: c.wait_send())
        for s in range(group - 1):
            sum_copy(s, r).wait_send()
            field_copy_to(s, r, me).wait_send()


def correct(back, field, taps, wm, inv, last):
    views, depth, ny, nz = back.shape
    group = lax.axis_size("view")
    reach = taps.shape[-1] // 2
    pad = reach + 1
    piece = ny // group
    rounds = piece // 8
    dma = pltpu.SemaphoreType.DMA
    smem = pl.BlockSpec(memory_space=pltpu.SMEM)
    anywhere = pl.BlockSpec(memory_space=pl.ANY)
    vmem = pl.BlockSpec(memory_space=pltpu.VMEM)
    scratch = [
        pltpu.VMEM((views, depth + 2 * pad, ny, nz), jnp.float32),
        pltpu.VMEM((depth, piece, nz), jnp.float32),
        pltpu.VMEM((group, depth, piece, nz), jnp.float32),
        pltpu.VMEM((max(1, group - 1), depth, piece, nz), jnp.float32),
        dma((3,)),
        dma((2, group, rounds)),
        dma((2, group, rounds)),
        dma((group, rounds)),
        dma((group, rounds)),
        dma((group, rounds)),
        dma((group, rounds)),
    ]
    field_shape = jax.ShapeDtypeStruct((depth, ny, nz), jnp.float32)
    along_shape = jax.ShapeDtypeStruct((views, depth, ny, nz), jnp.float32)
    if not last:
        scratch += [
            pltpu.VMEM((depth + 2 * pad, ny, nz), jnp.float32),
            dma((2, group, rounds)),
            dma((2, group, rounds)),
        ]
    return pl.pallas_call(
        functools.partial(correct_kernel, last, reach),
        out_shape=field_shape if last else (field_shape, along_shape),
        in_specs=[anywhere, anywhere, smem, smem, smem],
        out_specs=vmem if last else (anywhere, vmem),
        scratch_shapes=scratch,
        compiler_params=pltpu.CompilerParams(
            collective_id=1 if last else 0,
            has_side_effects=True,
            vmem_limit_bytes=48 * 1024 * 1024,
        ),
        name="correct_last" if last else "correct_mid",
    )(back, field, taps, wm, inv)


def banded_blur_matrix(filter_tap_values, row_count, col_count, offset_base, orientation):
    tap_count = filter_tap_values.shape[-1]
    grid_shape = (row_count, col_count, tap_count)
    row_index = lax.broadcasted_iota(jnp.int32, grid_shape, 0)
    col_index = lax.broadcasted_iota(jnp.int32, grid_shape, 1)
    tap_index = lax.broadcasted_iota(jnp.int32, grid_shape, 2)
    selected_entries = (orientation * (row_index - col_index) + offset_base == tap_index).astype(
        jnp.float32
    )
    return jnp.einsum(
        "ewq,gq->gew", selected_entries, filter_tap_values, precision=lax.Precision.HIGHEST
    )


def on_device(
    estimate, observed, route_dest, route_pos, view_span, view_count, psf_taps, view_weight
):
    highest = lax.Precision.HIGHEST
    blocks = lax.axis_size("block")
    slot_count = observed.shape[1]
    planes = observed.shape[2]
    ny_cells = observed.shape[3]
    nz_cells = observed.shape[4]
    per_group = view_span.shape[0]
    per_block = view_count.shape[0]
    capacity = max(1, slot_count // blocks)
    block_x = per_block * planes
    reach = psf_taps.shape[-1] // 2
    sources = observed[0]
    dest_list = route_dest[0]
    pos_list = route_pos[0]
    slot_index = jnp.arange(slot_count, dtype=jnp.int32)
    earlier = (dest_list[:, None] == dest_list[None, :]) & (
        slot_index[None, :] < slot_index[:, None]
    )
    rank_in_dest = jnp.sum(earlier.astype(jnp.int32), axis=1)
    target = jnp.where(dest_list >= 0, dest_list * capacity + rank_in_dest, blocks * capacity)
    outgoing = (
        jnp.zeros((blocks * capacity, planes, ny_cells, nz_cells), jnp.float32)
        .at[target]
        .set(sources, mode="drop")
    )
    out_pos = (
        jnp.full((blocks * capacity,), -1.0, jnp.float32)
        .at[target]
        .set(pos_list.astype(jnp.float32), mode="drop")
    )
    padded = with_halo(estimate, (("block", 0),), reach)
    padded, outgoing = lax.optimization_barrier((padded, outgoing))
    arrived, arrived_pos = (
        lax.all_to_all(
            outgoing.reshape(blocks, capacity, planes, ny_cells, nz_cells),
            "block",
            split_axis=0,
            concat_axis=0,
            tiled=True,
        ),
        lax.all_to_all(
            out_pos.reshape(blocks, capacity), "block", split_axis=0, concat_axis=0, tiled=True
        ),
    )
    places = arrived_pos.reshape(-1).astype(jnp.int32)
    places = jnp.where(places >= 0, places, per_group * per_block)
    placed = (
        jnp.zeros((per_group * per_block, planes, ny_cells, nz_cells), jnp.float32)
        .at[places]
        .set(arrived.reshape(-1, planes, ny_cells, nz_cells), mode="drop")
    )
    obs_views = placed.reshape(per_group, block_x, ny_cells, nz_cells)
    brick_index = lax.axis_index("block") * per_block + jnp.arange(per_block, dtype=jnp.int32)
    span_first = view_span[:, 0:1]
    span_length = view_span[:, 1:2]
    inside = (
        (brick_index[None, :] >= span_first) & (brick_index[None, :] < span_first + span_length)
    ).astype(jnp.float32)
    live_cells = jnp.repeat(inside, planes, axis=1)[:, :, None, None]
    point_spread_kernels = psf_taps / jnp.sum(psf_taps, axis=-1, keepdims=True)
    fwd_x = banded_blur_matrix(point_spread_kernels[:, 0], block_x + 2 * reach, block_x, 0, 1)
    mat_y = banded_blur_matrix(point_spread_kernels[:, 1], ny_cells, ny_cells, reach, 1)
    mat_z = banded_blur_matrix(point_spread_kernels[:, 2], nz_cells, nz_cells, reach, 1)
    wm = jnp.repeat(inside, planes, axis=1) * view_weight[:, None]
    inv = (1.0 / jnp.repeat(view_count.astype(jnp.float32), planes))[None, :]
    taps_x = point_spread_kernels[:, 0]
    current = estimate
    along_x = jnp.einsum("wyz,vwx->vxyz", padded, fwd_x, precision=highest)
    for iteration in range(ITERS):
        lateral_y_pass = jnp.einsum("vxyz,vyq->vxqz", along_x, mat_y, precision=PREC)
        blurred = jnp.einsum("vxyz,vzq->vxyq", lateral_y_pass, mat_z, precision=PREC)
        ratios = live_cells * (obs_views / blurred) + (1.0 - live_cells)
        back_z = jnp.einsum("vxyz,vqz->vxyq", ratios, mat_z, precision=PREC)
        back_y = jnp.einsum("vxyz,vqy->vxqz", back_z, mat_y, precision=PREC)
        if iteration < ITERS - 1:
            current, along_x = correct(back_y, current, taps_x, wm, inv, False)
        else:
            current = correct(back_y, current, taps_x, wm, inv, True)
    return current


def solution(mesh):
    placed = (
        P("block", None, None),
        P("view", "block", None, None, None),
        P("view", "block"),
        P("view", "block"),
        P("view", None),
        P("block"),
        P("view", None, None),
        P("view"),
    )
    return jax.shard_map(
        on_device, mesh=mesh, in_specs=placed, out_specs=P("block", None, None), check_vma=False
    )
```

```python
import functools

import jax
import jax.numpy as jnp
from jax import lax
from jax.experimental import pallas as pl
from jax.experimental.pallas import tpu as pltpu
from jax.sharding import PartitionSpec as P

ITERS = 2
PREC = lax.Precision.HIGH


def halo_planes(cells, axis, width):
    count = lax.axis_size(axis)
    ends = count - 1
    return (
        lax.ppermute(cells[-width:], axis, [(i, (i + 1) % count) for i in range(ends)]),
        lax.ppermute(cells[:width], axis, [((i + 1) % count, i) for i in range(ends)]),
    )


def ratio_kernel(slot_ref, filled_ref, live_ref, arrived_ref, blurred_ref, ratio_ref, placed_ref):
    i = pl.program_id(0)
    seen = jnp.where(filled_ref[i] > 0, arrived_ref[...], 0.0)
    placed_ref[...] = seen
    ratio_ref[...] = live_ref[i] * (seen / blurred_ref[...]) + (1.0 - live_ref[i])


def placed_ratio(slot, filled, live, arrived, blurred):
    brick = (1, *arrived.shape[1:])
    here = pl.BlockSpec(brick, lambda i, *_: (i, 0, 0, 0))
    shape = jax.ShapeDtypeStruct((slot.shape[0], *arrived.shape[1:]), jnp.float32)
    return pl.pallas_call(
        ratio_kernel,
        grid_spec=pltpu.PrefetchScalarGridSpec(
            num_scalar_prefetch=3,
            grid=(slot.shape[0],),
            in_specs=[pl.BlockSpec(brick, lambda i, slot, *_: (slot[i], 0, 0, 0)), here],
            out_specs=[here, here],
        ),
        out_shape=[shape, shape],
        compiler_params=pltpu.CompilerParams(vmem_limit_bytes=16 * 1024 * 1024),
        name="placed_ratio",
    )(slot, filled, live, arrived, blurred)


MESH = pl.DeviceIdType.MESH


def blur_tile(src, lead, taps_ref, view, rows, lanes, depth, first, step):
    total = None
    for t in range(taps_ref.shape[1]):
        start = first + step * t
        term = taps_ref[view, t] * src[(*lead, pl.ds(start, depth), rows, lanes)]
        total = term if total is None else total + term
    return total


def correct_kernel(last, reach, *refs):
    if last:
        (back_ref, f_ref, taps_ref, wm_ref, inv_ref, fout_ref,
         ext, own, part, rs, in_sem, rh_send, rh_recv, rs_send, rs_recv, ag_send, ag_recv) = refs
        fb, fbase = fout_ref, 0
    else:
        (back_ref, f_ref, taps_ref, wm_ref, inv_ref, fout_ref, along_ref,
         ext, own, part, rs, in_sem, rh_send, rh_recv, rs_send, rs_recv, ag_send, ag_recv,
         fext, fh_send, fh_recv) = refs
        fb, fbase = fext, reach + 1
    views, depth = back_ref.shape[0], back_ref.shape[1]
    ny, nz = back_ref.shape[2], back_ref.shape[3]
    pad = reach + 1
    group = lax.axis_size("view")
    blocks = lax.axis_size("block")
    me = lax.axis_index("view")
    blk = lax.axis_index("block")
    piece = ny // group
    has_left = blk > 0
    has_right = blk < blocks - 1

    part_rows = 8
    rounds = piece // part_rows

    def rows_of(p):
        return pl.ds(pl.multiple_of(p * piece, piece), piece)

    def rows_at(p, r):
        return pl.ds(pl.multiple_of(p * piece + r * part_rows, part_rows), part_rows)

    def inner_at(r):
        return pl.ds(pl.multiple_of(r * part_rows, part_rows), part_rows)

    centre = pltpu.make_async_copy(back_ref, ext.at[:, pl.ds(pad, depth)], in_sem.at[0])
    centre.start()
    mine = pltpu.make_async_copy(
        f_ref.at[:, rows_of(me)], own, in_sem.at[1]
    )
    mine.start()

    barrier = pltpu.get_barrier_semaphore()
    for s in range(group - 1):
        pl.semaphore_signal(
            barrier, inc=1, device_id=(lax.rem(me + 1 + s, group), blk), device_id_type=MESH
        )

    @pl.when(has_left)
    def _():
        pl.semaphore_signal(barrier, inc=1, device_id=(me, blk - 1), device_id_type=MESH)

    @pl.when(has_right)
    def _():
        pl.semaphore_signal(barrier, inc=1, device_id=(me, blk + 1), device_id_type=MESH)

    @pl.when(blk == 0)
    def _():
        ext[:, 0:pad] = jnp.zeros((views, pad, ny, nz), jnp.float32)
        if not last:
            fext[0:pad] = jnp.zeros((pad, ny, nz), jnp.float32)

    @pl.when(blk == blocks - 1)
    def _():
        ext[:, pad + depth:] = jnp.zeros((views, pad, ny, nz), jnp.float32)
        if not last:
            fext[pad + depth:] = jnp.zeros((pad, ny, nz), jnp.float32)

    pl.semaphore_wait(
        barrier, group - 1 + has_left.astype(jnp.int32) + has_right.astype(jnp.int32)
    )
    centre.wait()

    def ratio_copy(side, s, r):
        rows = rows_at(lax.rem(me + 1 + s, group), r)
        src0, dst0 = (pad + depth - reach, pad - reach) if side == 0 else (pad, pad + depth)
        return pltpu.make_async_remote_copy(
            src_ref=ext.at[:, pl.ds(src0, reach), rows],
            dst_ref=ext.at[:, pl.ds(dst0, reach), rows],
            send_sem=rh_send.at[side, s, r],
            recv_sem=rh_recv.at[side, s, r],
            device_id=(me, blk + 1 if side == 0 else blk - 1),
            device_id_type=MESH,
        )

    def field_copy(side, k, r):
        p = me if k == 0 else lax.rem(me - k + group, group)
        rows = rows_at(p, r)
        src0, dst0 = (pad + depth - reach, pad - reach) if side == 0 else (pad, pad + depth)
        return pltpu.make_async_remote_copy(
            src_ref=fext.at[pl.ds(src0, reach), rows],
            dst_ref=fext.at[pl.ds(dst0, reach), rows],
            send_sem=fh_send.at[side, k, r],
            recv_sem=fh_recv.at[side, k, r],
            device_id=(me, blk + 1 if side == 0 else blk - 1),
            device_id_type=MESH,
        )

    def to_sides(make, k, r, act):
        @pl.when(has_right)
        def _():
            act(make(0, k, r))

        @pl.when(has_left)
        def _():
            act(make(1, k, r))

    def from_sides(make, k, r):
        @pl.when(has_left)
        def _():
            make(0, k, r).wait_recv()

        @pl.when(has_right)
        def _():
            make(1, k, r).wait_recv()

    def each_round(act):
        def step(r, carry):
            act(r)
            return carry

        lax.fori_loop(0, rounds, step, 0)

    @each_round
    def _(r):
        for s in range(group):
            to_sides(ratio_copy, s, r, lambda c: c.start())

    tiles = nz // 128

    def lanes_at(i):
        return pl.ds(pl.multiple_of(i * 128, 128), 128)

    def sum_copy(s, r):
        return pltpu.make_async_remote_copy(
            src_ref=part.at[s, :, inner_at(r)],
            dst_ref=rs.at[s, :, inner_at(r)],
            send_sem=rs_send.at[s, r],
            recv_sem=rs_recv.at[s, r],
            device_id=(lax.rem(me + 1 + s, group), blk),
            device_id_type=MESH,
        )

    def field_copy_to(s, r, p):
        where = fb.at[pl.ds(fbase, depth), rows_at(p, r)]
        return pltpu.make_async_remote_copy(
            src_ref=where,
            dst_ref=where,
            send_sem=ag_send.at[s, r],
            recv_sem=ag_recv.at[s, r],
            device_id=(lax.rem(me + 1 + s, group), blk),
            device_id_type=MESH,
        )

    def take_gathered(r):
        for s in range(group - 1):
            field_copy_to(s, r, lax.rem(me - 1 - s + group, group)).wait_recv()
            if not last:
                to_sides(field_copy, s + 1, r, lambda c: c.start())

    mine.wait()

    @each_round
    def _(r):
        inner = inner_at(r)
        for s in range(group):
            rows = rows_at(lax.rem(me + 1 + s, group), r)
            from_sides(ratio_copy, s, r)

            def body(i, carry, rows=rows, s=s):
                lanes = lanes_at(i)
                logs = [
                    jnp.log(
                        blur_tile(ext, (v,), taps_ref, v, rows, lanes, depth, pad + reach, -1)
                    )
                    for v in range(views)
                ]
                for x in range(depth):
                    total = wm_ref[0, x] * logs[0][x]
                    for v in range(1, views):
                        total = total + wm_ref[v, x] * logs[v][x]
                    part[s, x, inner, lanes] = total
                return carry

            lax.fori_loop(0, tiles, body, 0)
            if s < group - 1:
                sum_copy(s, r).start()

        for s in range(group - 1):
            sum_copy(s, r).wait_recv()
        rows = rows_at(me, r)

        def update(i, carry):
            lanes = lanes_at(i)
            for x in range(depth):
                total = part[group - 1, x, inner, lanes]
                for s in range(group - 1):
                    total = total + rs[s, x, inner, lanes]
                fb[fbase + x, rows, lanes] = own[x, inner, lanes] * jnp.exp(
                    total * inv_ref[0, x]
                )
            return carry

        lax.fori_loop(0, tiles, update, 0)
        for s in range(group - 1):
            field_copy_to(s, r, me).start()
        if not last:
            to_sides(field_copy, 0, r, lambda c: c.start())

        @pl.when(r > 0)
        def _():
            take_gathered(r - 1)

    take_gathered(rounds - 1)
    if not last:
        done = pltpu.make_async_copy(fext.at[pl.ds(pad, depth)], fout_ref, in_sem.at[2])
        done.start()

        @each_round
        def _(r):
            for k in range(group):
                rows = rows_at(me if k == 0 else lax.rem(me - k + group, group), r)
                from_sides(field_copy, k, r)

                def forward(i, carry, rows=rows):
                    lanes = lanes_at(i)
                    for v in range(views):
                        along_ref[v, :, rows, lanes] = blur_tile(
                            fext, (), taps_ref, v, rows, lanes, depth, pad - reach, 1
                        )
                    return carry

                lax.fori_loop(0, tiles, forward, 0)

        done.wait()

    @each_round
    def _(r):
        for s in range(group):
            to_sides(ratio_copy, s, r, lambda c: c.wait_send())
            if not last:
                to_sides(field_copy, s, r, lambda c: c.wait_send())
        for s in range(group - 1):
            sum_copy(s, r).wait_send()
            field_copy_to(s, r, me).wait_send()


def correct(back, field, taps, wm, inv, last):
    views, depth, ny, nz = back.shape
    group = lax.axis_size("view")
    reach = taps.shape[-1] // 2
    pad = reach + 1
    piece = ny // group
    rounds = piece // 8
    dma = pltpu.SemaphoreType.DMA
    smem = pl.BlockSpec(memory_space=pltpu.SMEM)
    anywhere = pl.BlockSpec(memory_space=pl.ANY)
    vmem = pl.BlockSpec(memory_space=pltpu.VMEM)
    scratch = [
        pltpu.VMEM((views, depth + 2 * pad, ny, nz), jnp.float32),
        pltpu.VMEM((depth, piece, nz), jnp.float32),
        pltpu.VMEM((group, depth, piece, nz), jnp.float32),
        pltpu.VMEM((max(1, group - 1), depth, piece, nz), jnp.float32),
        dma((3,)),
        dma((2, group, rounds)),
        dma((2, group, rounds)),
        dma((group, rounds)),
        dma((group, rounds)),
        dma((group, rounds)),
        dma((group, rounds)),
    ]
    field_shape = jax.ShapeDtypeStruct((depth, ny, nz), jnp.float32)
    along_shape = jax.ShapeDtypeStruct((views, depth, ny, nz), jnp.float32)
    if not last:
        scratch += [
            pltpu.VMEM((depth + 2 * pad, ny, nz), jnp.float32),
            dma((2, group, rounds)),
            dma((2, group, rounds)),
        ]
    return pl.pallas_call(
        functools.partial(correct_kernel, last, reach),
        out_shape=field_shape if last else (field_shape, along_shape),
        in_specs=[anywhere, anywhere, smem, smem, smem],
        out_specs=vmem if last else (anywhere, vmem),
        scratch_shapes=scratch,
        compiler_params=pltpu.CompilerParams(
            collective_id=1 if last else 0,
            has_side_effects=True,
            vmem_limit_bytes=48 * 1024 * 1024,
        ),
        name="correct_last" if last else "correct_mid",
    )(back, field, taps, wm, inv)


def banded_blur_matrix(filter_tap_values, row_count, col_count, offset_base, orientation):
    tap_count = filter_tap_values.shape[-1]
    grid_shape = (row_count, col_count, tap_count)
    row_index = lax.broadcasted_iota(jnp.int32, grid_shape, 0)
    col_index = lax.broadcasted_iota(jnp.int32, grid_shape, 1)
    tap_index = lax.broadcasted_iota(jnp.int32, grid_shape, 2)
    selected_entries = (orientation * (row_index - col_index) + offset_base == tap_index).astype(
        jnp.float32
    )
    return jnp.einsum(
        "ewq,gq->gew", selected_entries, filter_tap_values, precision=lax.Precision.HIGHEST
    )


def on_device(
    estimate, observed, route_dest, route_pos, view_span, view_count, psf_taps, view_weight
):
    highest = lax.Precision.HIGHEST
    blocks = lax.axis_size("block")
    slot_count = observed.shape[1]
    planes = observed.shape[2]
    ny_cells = observed.shape[3]
    nz_cells = observed.shape[4]
    per_group = view_span.shape[0]
    per_block = view_count.shape[0]
    capacity = max(1, slot_count // blocks)
    block_x = per_block * planes
    reach = psf_taps.shape[-1] // 2
    sources = observed[0]
    dest_list = route_dest[0]
    pos_list = route_pos[0]
    slot_index = jnp.arange(slot_count, dtype=jnp.int32)
    earlier = (dest_list[:, None] == dest_list[None, :]) & (
        slot_index[None, :] < slot_index[:, None]
    )
    rank_in_dest = jnp.sum(earlier.astype(jnp.int32), axis=1)
    target = jnp.where(dest_list >= 0, dest_list * capacity + rank_in_dest, blocks * capacity)
    outgoing = (
        jnp.zeros((blocks * capacity, planes, ny_cells, nz_cells), jnp.float32)
        .at[target]
        .set(sources, mode="drop")
    )
    out_pos = (
        jnp.full((blocks * capacity,), -1.0, jnp.float32)
        .at[target]
        .set(pos_list.astype(jnp.float32), mode="drop")
    )
    below, above, outgoing = lax.optimization_barrier(
        (*halo_planes(estimate, "block", reach), outgoing)
    )
    padded = jnp.concatenate([below, estimate, above], axis=0)
    arrived, arrived_pos = (
        lax.all_to_all(
            outgoing.reshape(blocks, capacity, planes, ny_cells, nz_cells),
            "block",
            split_axis=0,
            concat_axis=0,
            tiled=True,
        ),
        lax.all_to_all(
            out_pos.reshape(blocks, capacity), "block", split_axis=0, concat_axis=0, tiled=True
        ),
    )
    places = arrived_pos.reshape(-1).astype(jnp.int32)
    matches = places[None, :] == jnp.arange(per_group * per_block, dtype=jnp.int32)[:, None]
    filled = jnp.max(matches.astype(jnp.int32), axis=1)
    slot = jnp.max(
        jnp.where(matches, jnp.arange(places.shape[0], dtype=jnp.int32)[None, :], 0), axis=1
    )
    bricks = (per_group * per_block, planes, ny_cells, nz_cells)
    views = (per_group, block_x, ny_cells, nz_cells)
    brick_index = lax.axis_index("block") * per_block + jnp.arange(per_block, dtype=jnp.int32)
    span_first = view_span[:, 0:1]
    span_length = view_span[:, 1:2]
    inside = (
        (brick_index[None, :] >= span_first) & (brick_index[None, :] < span_first + span_length)
    ).astype(jnp.float32)
    live_cells = jnp.repeat(inside, planes, axis=1)[:, :, None, None]
    point_spread_kernels = psf_taps / jnp.sum(psf_taps, axis=-1, keepdims=True)
    fwd_x = banded_blur_matrix(point_spread_kernels[:, 0], block_x + 2 * reach, block_x, 0, 1)
    mat_y = banded_blur_matrix(point_spread_kernels[:, 1], ny_cells, ny_cells, reach, 1)
    mat_z = banded_blur_matrix(point_spread_kernels[:, 2], nz_cells, nz_cells, reach, 1)
    wm = jnp.repeat(inside, planes, axis=1) * view_weight[:, None]
    inv = (1.0 / jnp.repeat(view_count.astype(jnp.float32), planes))[None, :]
    taps_x = point_spread_kernels[:, 0]
    current = estimate
    along_x = jnp.einsum("wyz,vwx->vxyz", padded, fwd_x, precision=highest)
    for iteration in range(ITERS):
        lateral_y_pass = jnp.einsum("vxyz,vyq->vxqz", along_x, mat_y, precision=PREC)
        blurred = jnp.einsum("vxyz,vzq->vxyq", lateral_y_pass, mat_z, precision=PREC)
        if iteration == 0:
            ratios, placed = placed_ratio(
                slot,
                filled,
                inside.reshape(-1),
                arrived.reshape(-1, planes, ny_cells, nz_cells),
                blurred.reshape(bricks),
            )
            ratios, obs_views = ratios.reshape(views), placed.reshape(views)
        else:
            ratios = live_cells * (obs_views / blurred) + (1.0 - live_cells)
        back_z = jnp.einsum("vxyz,vqz->vxyq", ratios, mat_z, precision=PREC)
        back_y = jnp.einsum("vxyz,vqy->vxqz", back_z, mat_y, precision=PREC)
        if iteration < ITERS - 1:
            current, along_x = correct(back_y, current, taps_x, wm, inv, False)
        else:
            current = correct(back_y, current, taps_x, wm, inv, True)
    return current


def solution(mesh):
    placed = (
        P("block", None, None),
        P("view", "block", None, None, None),
        P("view", "block"),
        P("view", "block"),
        P("view", None),
        P("block"),
        P("view", None, None),
        P("view"),
    )
    return jax.shard_map(
        on_device, mesh=mesh, in_specs=placed, out_specs=P("block", None, None), check_vma=False
    )
```
